32 devices in a mesh: grp: 4 (over y, x), tok: 4 (over z), mdl: 2 (over core).
Axes of the slice: x: 2, y: 2, z: 4, core: 2. Of those that a mesh axis runs over, the one named last changes fastest.
Arguments:
- hidden_in: bfloat16 [4, 512, 5120], P('grp', 'tok', 'mdl'), may hold values from -8 to 8
- seg_ids: int32 [4, 512], replicated, may hold values from 0 to 3, never falling along the last dimension, each value on 1 to 384 neighbouring positions
- request_prefix: int32 [4, 4], replicated, may hold values from 0 to 1
- page_table: int32 [32], replicated, may hold values from 0 to 31, each once
- prefix_cache: bfloat16 [32, 256, 8, 256], P(('grp', 'mdl'), None, 'tok'), may hold values from -200 to 200
- attn_gain: float32 [5120], P('mdl'), may hold values from 0.1 to 1.9
- w_query: bfloat16 [5120, 5120], P('mdl', 'tok'), may hold values from -0.078125 to 0.078125
- w_key: bfloat16 [5120, 1024], P('mdl', 'tok'), may hold values from -0.25 to 0.25
- w_value: bfloat16 [5120, 1024], P('mdl', 'tok'), may hold values from -0.078125 to 0.078125
- w_out: bfloat16 [5120, 5120], P('tok', 'mdl'), may hold values from -0.078125 to 0.078125
- ffn_gain: float32 [5120], P('mdl'), may hold values from 0.1 to 1.9
- w_gate: bfloat16 [5120, 14336], P('mdl', 'tok'), may hold values from -0.078125 to 0.078125
- w_up: bfloat16 [5120, 14336], P('mdl', 'tok'), may hold values from -0.078125 to 0.078125
- w_down: bfloat16 [14336, 5120], P('tok', 'mdl'), may hold values from -0.046875 to 0.046875
- final_gain: float32 [5120], replicated, may hold values from 0.1 to 1.9
- lm_head: bfloat16 [76800, 5120], P(('grp', 'tok', 'mdl')), may hold values from -0.25 to 0.25
Outputs:
- hidden_out: bfloat16 [4, 512, 5120], P('grp', 'tok', 'mdl')
- new_kv: bfloat16 [4, 512, 8, 256], P('grp', 'mdl', 'tok')
- req_norm: float32 [4, 4], P('grp')
- max_logit: float32 [4, 4], replicated
- logits: float32 [16, 76800], P(None, ('grp', 'tok', 'mdl'))
The draws below stay inside these ranges and needn't reach their ends.
Inputs may be any that keep to these rules, and one draw needn't show every extreme that they name: `seg_ids`: requests of a group are contiguous, in order, and none is empty. `page_table`: each physical slot holds exactly one logical page.
All inputs are finite; a program needn't handle non-finite values.
Results may differ from the reference program's by a relative error of at most 0.024.
Values may be sent and summed in bfloat16 or wider, within the bound.
A program may use at most 256 MiB of HBM per device.

```python
import math
import jax
import jax.numpy as jnp
import numpy as np
from jax import lax

D = 5120
HEADS = 40
KVH = 8
HD = 128
FF = 14336
VOCAB = 76800
NPREFIX = 2
PREFIX = 4096
PAGE = 256
REQ = 4
SEQ = 512
SLOTS = 32
N_GRP = 4
N_MDL = 2


def draw_hidden_in(key, part):
    full_shape = (N_GRP, SEQ, D)
    feature = jnp.arange(D, dtype=jnp.float32) / (D - 1)
    base_values = jnp.clip(jax.random.normal(key, full_shape, jnp.float32), -4.0, 4.0)
    scale_row = 0.6 * jnp.exp(feature * 1.0986123)
    return (base_values * scale_row[None, None, :]).astype(jnp.bfloat16)


def draw_prefix_cache(key, part):
    base_key = jax.random.fold_in(key, 0)
    full_shape = (SLOTS, PAGE, KVH, 2 * HD)
    base_values = jnp.clip(jax.random.normal(base_key, full_shape, jnp.float32), -6.0, 6.0)
    key_part = base_values[..., :HD] * 3.0
    value_part = base_values[..., HD:]
    return jnp.concatenate([key_part, value_part], -1).astype(jnp.bfloat16)


def plant(values, stream_key, least, largest):
    longest = values.shape.index(max(values.shape))
    spots = []
    for shift in (0, 1):
        where = [jax.random.randint(jax.random.fold_in(stream_key, axis), (), 0, length) for axis, length in enumerate(values.shape)]
        where[longest] = (where[longest] + shift) % values.shape[longest]
        spots.append(tuple(where))
    return values.at[spots[0]].set(least).at[spots[1]].set(largest)


def level_of(own_key, extent, cuts, low, top_value):
    factor_of, own = 1.0, jax.random.fold_in(own_key, 6)
    for dim, blocks in cuts:
        draws = jnp.exp(jax.random.uniform(jax.random.fold_in(own, dim), (blocks,), jnp.float32, low / len(cuts), top_value / len(cuts)))
        factor_of = factor_of * jnp.repeat(draws, extent[dim] // blocks).reshape([-1 if axis == dim else 1 for axis in range(len(extent))])
    return factor_of


def split_up(count, total, most, skew):
    loads = [(1 << 20) // math.isqrt(rank ** skew) + 1 for rank in range(2, count + 1)]
    surplus, given = total - most - (count - 1), [1] * (count - 1)
    while surplus > 0:
        free = [i for i in range(count - 1) if given[i] < most]
        pool, budget = sum([loads[i] for i in free]), surplus
        for i in free:
            more = min(most - given[i], max(1, budget * loads[i] // pool), surplus)
            given[i] = given[i] + more
            surplus = surplus - more
    return np.array([most] + given)


def uneven_parts(rng, number_of, total, limit, slope):
    if number_of == 2:
        one = jax.random.randint(rng, (), max(1, total - limit), min(limit, total - 1) + 1)
        return jnp.stack([one, total - one])
    tallies = jnp.asarray(split_up(number_of, total, limit, slope), jnp.int32)
    couples = (number_of - 1) // 2
    source_of, sink = tallies[1:1 + 2 * couples:2], tallies[2:2 + 2 * couples:2]
    margin = jnp.minimum(source_of - 1, limit - sink)
    shifted = jax.random.randint(jax.random.fold_in(rng, 1), (couples,), 0, 1 << 20) % (margin + 1)
    tallies = tallies.at[1:1 + 2 * couples:2].set(source_of - shifted).at[2:2 + 2 * couples:2].set(sink + shifted)
    return tallies[jax.random.permutation(jax.random.fold_in(rng, 2), number_of)]


def scatter_about(stream_key, extent, width, limit, cuts=(), kind=jnp.bfloat16):
    values = jax.random.normal(stream_key, extent, jnp.float32) * width
    if len(cuts) > 0:
        values = level_of(stream_key, extent, cuts, -0.22, 0.18) * values
    return jnp.clip(values, min=-limit, max=limit).astype(kind)


def setup_inputs(seed: int = 0) -> dict:
    key_of = jax.random.split(jax.random.key(seed), 17)
    return {
        "hidden_in": draw_hidden_in(jax.random.fold_in(key_of[16], 71), 0),
        "seg_ids": jax.vmap(lambda own: jnp.searchsorted(jnp.cumsum(uneven_parts(own, REQ, SEQ, SEQ * 3 // 4, 2)), jnp.arange(SEQ), side="right"))(jax.random.split(key_of[1], N_GRP)).reshape((N_GRP, SEQ)).astype(jnp.int32),
        "request_prefix": plant(jax.random.randint(key_of[2], (N_GRP, REQ), 0, NPREFIX), jax.random.fold_in(key_of[2], 1), 0, NPREFIX - 1).astype(jnp.int32),
        "page_table": jax.random.permutation(key_of[3], SLOTS).astype(jnp.int32),
        "prefix_cache": draw_prefix_cache(jax.random.fold_in(key_of[16], 71), 0),
        "attn_gain": jnp.clip(1.0 + 0.18 * jax.random.normal(key_of[5], (D,), jnp.float32), 0.1, 1.9),
        "w_query": scatter_about(key_of[6], (D, HEADS * HD), D ** -0.5, 0.078125, ((0, 2), (1, 4))),
        "w_key": scatter_about(key_of[7], (D, KVH * HD), (D // 9) ** -0.5, 0.25, ((0, 2), (1, 4))),
        "w_value": scatter_about(key_of[8], (D, KVH * HD), D ** -0.5, 0.078125, ((0, 2), (1, 4))),
        "w_out": scatter_about(key_of[9], (HEADS * HD, D), (HEADS * HD) ** -0.5, 0.078125, ((0, 4), (1, 2))),
        "ffn_gain": jnp.clip(1.0 + 0.18 * jax.random.normal(key_of[10], (D,), jnp.float32), 0.1, 1.9),
        "w_gate": scatter_about(key_of[11], (D, FF), D ** -0.5, 0.078125, ((0, 2), (1, 4))),
        "w_up": scatter_about(key_of[12], (D, FF), D ** -0.5, 0.078125, ((0, 2), (1, 4))),
        "w_down": scatter_about(key_of[13], (FF, D), FF ** -0.5, 0.046875, ((0, 4), (1, 2))),
        "final_gain": jnp.clip(1.0 + 0.18 * jax.random.normal(key_of[14], (D,), jnp.float32), 0.1, 1.9),
        "lm_head": scatter_about(key_of[15], (VOCAB, D), (D // 9) ** -0.5, 0.25, ((0, 32),)),
    }


EPS = 1e-06
THETA = 1000000.0
NEG = -1e+30

def rotate(tensor, positions):
    half_dim = tensor.shape[-1] // 2
    frequency = THETA ** (-(jnp.arange(half_dim, dtype=jnp.float32) * 2.0 / tensor.shape[-1]))
    angles = positions.astype(jnp.float32)[:, None] * frequency[None, :]
    cosine = jnp.cos(angles)[:, None, :]
    sine_part = jnp.sin(angles)[:, None, :]
    first_part = tensor[..., :half_dim]
    second = tensor[..., half_dim:]
    return jnp.concatenate([first_part * cosine - second * sine_part, second * cosine + first_part * sine_part], -1)

def group_layer(tokens, seg_row, prefix_row, slot_prefix, prefix_cache, attn_gain, w_query, w_key, w_value, w_out, ffn_gain, w_gate, w_up, w_down):
    group_size = HEADS // KVH
    score_scale = HD ** (-0.5)
    tok_f = tokens.astype(jnp.float32)
    normed = (tok_f * lax.rsqrt(lax.optimization_barrier(jnp.mean(tok_f * tok_f, -1, keepdims=True)) + EPS) * attn_gain).astype(jnp.bfloat16)
    queries = jnp.dot(normed, w_query, preferred_element_type=jnp.float32).reshape(SEQ, HEADS, HD)
    key_rows = jnp.dot(normed, w_key, preferred_element_type=jnp.float32).reshape(SEQ, KVH, HD)
    value_rows = jnp.dot(normed, w_value, preferred_element_type=jnp.float32).reshape(SEQ, KVH, HD)
    indices = jnp.arange(SEQ, dtype=jnp.int32)
    requests = jnp.arange(REQ, dtype=jnp.int32)
    member = seg_row[:, None] == requests[None, :]
    counts = lax.optimization_barrier(jnp.sum(member.astype(jnp.int32), 0))
    offsets = jnp.cumsum(counts) - counts
    positions = PREFIX + indices - offsets[seg_row]
    q_rot = rotate(queries, positions).astype(jnp.bfloat16)
    k_rot = rotate(key_rows, positions).astype(jnp.bfloat16)
    appended = jnp.concatenate([k_rot, value_rows.astype(jnp.bfloat16)], -1)
    row_prefix = prefix_row[seg_row]
    key_prefix = jnp.repeat(slot_prefix, PAGE)
    prefix_ok = (row_prefix[:, None] == key_prefix[None, :])[:, None, :]
    suffix_ok = ((seg_row[:, None] == seg_row[None, :]) & (indices[None, :] <= indices[:, None]))[:, None, :]

    def one_head(head_index):
        q_head = lax.dynamic_slice_in_dim(q_rot, head_index * group_size, group_size, 1).astype(jnp.float32)
        cache_head = lax.dynamic_index_in_dim(prefix_cache, head_index, 2, keepdims=False)
        cache_head = cache_head.reshape(SLOTS * PAGE, 2 * HD).astype(jnp.float32)
        suffix_head = lax.dynamic_index_in_dim(appended, head_index, 1, keepdims=False).astype(jnp.float32)
        pre_scores = jnp.einsum('sgd,kd->sgk', q_head, cache_head[:, :HD]) * score_scale
        suf_scores = jnp.einsum('sgd,td->sgt', q_head, suffix_head[:, :HD]) * score_scale
        pre_scores = jnp.where(prefix_ok, pre_scores, NEG)
        suf_scores = jnp.where(suffix_ok, suf_scores, NEG)
        row_max = jnp.maximum(lax.optimization_barrier(jnp.max(pre_scores, -1)), lax.optimization_barrier(jnp.max(suf_scores, -1)))
        pre_weights = jnp.where(prefix_ok, jnp.exp(pre_scores - row_max[..., None]), 0.0)
        suf_weights = jnp.where(suffix_ok, jnp.exp(suf_scores - row_max[..., None]), 0.0)
        row_total = lax.optimization_barrier(jnp.sum(pre_weights, -1)) + lax.optimization_barrier(jnp.sum(suf_weights, -1))
        pre_round = lax.optimization_barrier(pre_weights.astype(jnp.bfloat16)).astype(jnp.float32)
        suf_round = lax.optimization_barrier(suf_weights.astype(jnp.bfloat16)).astype(jnp.float32)
        mixed = jnp.einsum('sgk,kd->sgd', pre_round, cache_head[:, HD:]) + jnp.einsum('sgt,td->sgd', suf_round, suffix_head[:, HD:])
        return (mixed / row_total[..., None]).astype(jnp.bfloat16)
    heads_out = lax.map(one_head, jnp.arange(KVH, dtype=jnp.int32))
    attended = jnp.transpose(heads_out, (1, 0, 2, 3)).reshape(SEQ, HEADS * HD)
    residual = tok_f + jnp.dot(attended, w_out, preferred_element_type=jnp.float32)
    ffn_input = (residual * lax.rsqrt(lax.optimization_barrier(jnp.mean(residual * residual, -1, keepdims=True)) + EPS) * ffn_gain).astype(jnp.bfloat16)
    block_width = D // N_MDL
    gate = jnp.zeros((SEQ, FF), jnp.float32)
    up_sum = jnp.zeros((SEQ, FF), jnp.float32)
    for block in range(N_MDL):
        piece = ffn_input[:, block * block_width:(block + 1) * block_width]
        gate_part = jnp.dot(piece, w_gate[block * block_width:(block + 1) * block_width], preferred_element_type=jnp.float32)
        up_part = jnp.dot(piece, w_up[block * block_width:(block + 1) * block_width], preferred_element_type=jnp.float32)
        gate = gate + lax.optimization_barrier(gate_part.astype(jnp.bfloat16)).astype(jnp.float32)
        up_sum = up_sum + lax.optimization_barrier(up_part.astype(jnp.bfloat16)).astype(jnp.float32)
    hidden_units = (jax.nn.silu(gate) * up_sum).astype(jnp.bfloat16)
    final_rows = residual + jnp.dot(hidden_units, w_down, preferred_element_type=jnp.float32)
    row_squares = lax.optimization_barrier(jnp.sum(final_rows * final_rows, -1))
    req_squares = lax.optimization_barrier(jnp.sum(jnp.where(member, row_squares[:, None], 0.0), 0))
    req_norm = jnp.sqrt(req_squares / (counts.astype(jnp.float32) * D) + EPS)
    last_rows = final_rows[offsets + counts - 1]
    return (final_rows.astype(jnp.bfloat16), appended, req_norm, last_rows)

def reference(hidden_in, seg_ids, request_prefix, page_table, prefix_cache, attn_gain, w_query, w_key, w_value, w_out, ffn_gain, w_gate, w_up, w_down, final_gain, lm_head):
    pages_each = PREFIX // PAGE
    entries = jnp.arange(SLOTS, dtype=jnp.int32)
    slot_prefix = jnp.zeros((SLOTS,), jnp.int32).at[page_table].set(entries // pages_each)
    outputs = []
    appends = []
    norms = []
    lasts = []
    for group in range(hidden_in.shape[0]):
        result = group_layer(hidden_in[group], seg_ids[group], request_prefix[group], slot_prefix, prefix_cache, attn_gain, w_query, w_key, w_value, w_out, ffn_gain, w_gate, w_up, w_down)
        outputs.append(result[0])
        appends.append(result[1])
        norms.append(result[2])
        lasts.append(result[3])
    last_all = jnp.concatenate(lasts, 0)
    last_normed = (last_all * lax.rsqrt(lax.optimization_barrier(jnp.mean(last_all * last_all, -1, keepdims=True)) + EPS) * final_gain).astype(jnp.bfloat16)
    logits = lax.dot_general(last_normed, lm_head, (((1,), (1,)), ((), ())), preferred_element_type=jnp.float32)
    max_logit = lax.optimization_barrier(jnp.max(logits, -1)).reshape(hidden_in.shape[0], REQ)
    return (jnp.stack(outputs, 0), jnp.stack(appends, 0), jnp.stack(norms, 0), max_logit, logits)
```

```python
import functools

import jax
import jax.numpy as jnp
from jax import lax
from jax.experimental import pallas as pl
from jax.experimental.pallas import tpu as pltpu
from jax.sharding import PartitionSpec as P

PREFIX = 4096
PAGE = 256


EPS = 1e-06
THETA = 1000000.0
NEG = -1e30


MESH = pl.DeviceIdType.MESH
LOG2E = 1.4426950408889634


def turn(block, cosine, signed_sine):
    return block * cosine + pltpu.roll(block, block.shape[1] // 2, 1) * signed_sine


def rope_kv_body(k_ref, v_ref, cos_ref, sin_ref, out_ref):
    width = k_ref.shape[1]
    out_ref[:, :width] = turn(k_ref[...], cos_ref[...], sin_ref[...]).astype(jnp.bfloat16)
    out_ref[:, width:] = v_ref[...].astype(jnp.bfloat16)


def rope_kv(qkv_rows, cosine, sine, heads, kv_dev, head_dim):
    rows = qkv_rows.shape[0]
    return pl.pallas_call(
        rope_kv_body,
        grid=(kv_dev,),
        in_specs=[
            pl.BlockSpec((rows, head_dim), lambda c: (0, heads + c)),
            pl.BlockSpec((rows, head_dim), lambda c: (0, heads + kv_dev + c)),
            pl.BlockSpec((rows, head_dim), lambda c: (0, 0)),
            pl.BlockSpec((rows, head_dim), lambda c: (0, 0)),
        ],
        out_specs=pl.BlockSpec((rows, 2 * head_dim), lambda c: (0, c)),
        out_shape=jax.ShapeDtypeStruct((rows, kv_dev * 2 * head_dim), jnp.bfloat16),
    )(qkv_rows, qkv_rows, cosine, sine)


def attend_body(
    prefixes, pages_each, page_len, group_size, head_dim, together,
    table_ref, need_ref,
    q_ref, cos_ref, sin_ref, seg_ref, row_ref, prefix_ref, key_seg_ref, suffix_ref, pages_ref,
    out_ref,
):
    block = pl.program_id(1)
    toks = q_ref.shape[0]
    scale = head_dim ** (-0.5) * LOG2E
    contract = (((1,), (1,)), ((), ()))
    q = jnp.concatenate(
        [
            turn(q_ref[:, h * head_dim : (h + 1) * head_dim], cos_ref[...], sin_ref[...])
            for h in range(group_size)
        ],
        0,
    ).astype(jnp.bfloat16)
    stack = lambda column: jnp.concatenate([column] * group_size, 0)
    seg = stack(seg_ref[...])
    row = stack(row_ref[...])
    prefix = stack(prefix_ref[...])

    def fold(parts, op):
        width = head_dim
        pieces = [p[:, j : j + width] for p in parts for j in range(0, p.shape[1], width)]
        return functools.reduce(op, pieces)

    keys = suffix_ref[:, :head_dim]
    scores = lax.dot_general(q, keys, contract, preferred_element_type=jnp.float32) * scale
    index = lax.broadcasted_iota(jnp.int32, scores.shape, 1)
    scores = jnp.where((key_seg_ref[...] == seg) & (index <= row), scores, NEG)
    top = jnp.max(fold([scores], jnp.maximum), 1, keepdims=True)
    weights = jnp.exp2(scores - top)
    total = fold([weights], jnp.add)
    mixed = jnp.dot(
        weights.astype(jnp.bfloat16), suffix_ref[:, head_dim:], preferred_element_type=jnp.float32
    )
    for p in range(prefixes):
        seen = prefix == p

        def step(i, carry):
            top, total, mixed = carry
            starts = [
                pl.multiple_of(
                    table_ref[p * pages_each + i * together + u] * page_len, page_len
                )
                for u in range(together)
            ]
            scores = [
                lax.dot_general(
                    q,
                    pages_ref[pl.ds(start, page_len), :head_dim],
                    contract,
                    preferred_element_type=jnp.float32,
                )
                for start in starts
            ]
            best = jnp.max(fold(scores, jnp.maximum), 1, keepdims=True) * scale
            new_top = jnp.where(seen, jnp.maximum(top, best), top)
            shift = jnp.where(seen, new_top, -NEG)
            factor = jnp.exp2(top - new_top)
            weights = [jnp.exp2(s * scale - shift) for s in scores]
            total = total * factor + fold(weights, jnp.add)
            mixed = mixed * factor
            for start, w in zip(starts, weights):
                mixed = mixed + jnp.dot(
                    w.astype(jnp.bfloat16),
                    pages_ref[pl.ds(start, page_len), head_dim:],
                    preferred_element_type=jnp.float32,
                )
            return new_top, total, mixed

        trips = need_ref[block * prefixes + p] * (pages_each // together)
        top, total, mixed = lax.fori_loop(0, trips, step, (top, total, mixed))
    result = (mixed / jnp.sum(total, 1, keepdims=True)).astype(jnp.bfloat16)
    for h in range(group_size):
        out_ref[:, h * head_dim : (h + 1) * head_dim] = result[h * toks : (h + 1) * toks]


def attend(
    qkv_rows, cosine, sine, my_seg, my_rows, my_prefix, seg_row, suffix, pages, page_table,
    kv_dev, group_size, head_dim, page_len,
):
    rows = qkv_rows.shape[0]
    toks = 64
    blocks = rows // toks
    pages_each = PREFIX // PAGE
    prefixes = page_table.shape[0] // pages_each
    need = jnp.max(
        (my_prefix.reshape(blocks, toks)[:, None, :] == jnp.arange(prefixes)[None, :, None]).astype(
            jnp.int32
        ),
        -1,
    ).reshape(-1)
    seq_len = suffix.shape[0]
    q_width = group_size * head_dim
    by_row = lambda c, b, *_: (b, 0)
    by_kv = lambda c, b, *_: (0, c)
    by_both = lambda c, b, *_: (b, c)
    body = functools.partial(
        attend_body, prefixes, pages_each, page_len, group_size, head_dim, 4
    )
    elements = rows * kv_dev * group_size * (PREFIX + seq_len)
    return pl.pallas_call(
        body,
        grid_spec=pltpu.PrefetchScalarGridSpec(
            num_scalar_prefetch=2,
            grid=(kv_dev, blocks),
            in_specs=[
                pl.BlockSpec((toks, q_width), by_both),
                pl.BlockSpec((toks, head_dim), by_row),
                pl.BlockSpec((toks, head_dim), by_row),
                pl.BlockSpec((toks, 1), by_row),
                pl.BlockSpec((toks, 1), by_row),
                pl.BlockSpec((toks, 1), by_row),
                pl.BlockSpec((1, seq_len), lambda c, b, *_: (0, 0)),
                pl.BlockSpec((seq_len, 2 * head_dim), by_kv),
                pl.BlockSpec((pages.shape[0], 2 * head_dim), by_kv),
            ],
            out_specs=pl.BlockSpec((toks, q_width), by_both),
        ),
        out_shape=jax.ShapeDtypeStruct((rows, kv_dev * q_width), jnp.bfloat16),
        compiler_params=pltpu.CompilerParams(vmem_limit_bytes=48 * 1024 * 1024),
        cost_estimate=pl.CostEstimate(
            flops=4 * head_dim * elements, bytes_accessed=pages.size * 2, transcendentals=elements
        ),
    )(
        page_table, need, qkv_rows, cosine, sine, my_seg[:, None], my_rows[:, None],
        my_prefix[:, None], seg_row[None, :], suffix, pages,
    )


def exchange_body(
    sizes, summing,
    x_ref, out_ref, tok_slots, stage, all_slots, tok_send, tok_recv, all_send, all_recv,
):
    grp_n, tok_n, mdl_n = sizes
    g, t, m = (lax.axis_index(name) for name in ("grp", "tok", "mdl"))
    tok_peers = [
        (d, {"tok": lax.rem(t + d, tok_n)}) for d in range(1, tok_n)
    ]
    plane_peers = [
        (
            gd * mdl_n + md,
            {"grp": lax.rem(g + gd, grp_n), "mdl": lax.rem(m + md, mdl_n)},
        )
        for gd in range(grp_n)
        for md in range(mdl_n)
        if gd + md > 0
    ]
    barrier = pltpu.get_barrier_semaphore()
    for _, peer in tok_peers + plane_peers:
        pl.semaphore_signal(barrier, inc=1, device_id=peer, device_id_type=MESH)
    pl.semaphore_wait(barrier, len(tok_peers) + len(plane_peers))

    def spread(source, slots, mine, peers, send, recv):
        copies = [
            pltpu.make_async_remote_copy(
                src_ref=source,
                dst_ref=slots.at[mine],
                send_sem=send.at[d],
                recv_sem=recv.at[d],
                device_id=peer,
                device_id_type=MESH,
            )
            for d, peer in peers
        ]
        for copy in copies:
            copy.start()
        slots[mine] = source[...]
        for copy in copies:
            copy.wait()

    join = jnp.add if summing else jnp.maximum
    spread(x_ref, tok_slots, t, tok_peers, tok_send, tok_recv)
    stage[...] = functools.reduce(join, [tok_slots[k] for k in range(tok_n)])
    spread(stage, all_slots, g * mdl_n + m, plane_peers, all_send, all_recv)
    if summing:
        out_ref[...] = all_slots[...]
    else:
        out_ref[...] = functools.reduce(join, [all_slots[k] for k in range(grp_n * mdl_n)])


def exchange(values, summing):
    sizes = tuple(lax.axis_size(name) for name in ("grp", "tok", "mdl"))
    plane = sizes[0] * sizes[2]
    shape = values.shape
    return pl.pallas_call(
        functools.partial(exchange_body, sizes, summing),
        out_shape=jax.ShapeDtypeStruct((plane,) + shape if summing else shape, jnp.float32),
        in_specs=[pl.BlockSpec(memory_space=pltpu.VMEM)],
        out_specs=pl.BlockSpec(memory_space=pltpu.VMEM),
        scratch_shapes=[
            pltpu.VMEM((sizes[1],) + shape, jnp.float32),
            pltpu.VMEM(shape, jnp.float32),
            pltpu.VMEM((plane,) + shape, jnp.float32),
            pltpu.SemaphoreType.DMA((sizes[1],)),
            pltpu.SemaphoreType.DMA((sizes[1],)),
            pltpu.SemaphoreType.DMA((plane,)),
            pltpu.SemaphoreType.DMA((plane,)),
        ],
        compiler_params=pltpu.CompilerParams(
            collective_id=1 if summing else 2, has_side_effects=True
        ),
    )(values)


def on_device(
    hidden_in,
    seg_ids,
    request_prefix,
    page_table,
    prefix_cache,
    attn_gain,
    w_query,
    w_key,
    w_value,
    w_out,
    ffn_gain,
    w_gate,
    w_up,
    w_down,
    final_gain,
    lm_head,
):
    groups_total = seg_ids.shape[0]
    seq_len = seg_ids.shape[1]
    req_count = request_prefix.shape[1]
    tok_rows = hidden_in.shape[1]
    feat_dev = hidden_in.shape[2]
    model_width = feat_dev * lax.axis_size("mdl")
    head_dim = prefix_cache.shape[3] // 2
    kv_dev = prefix_cache.shape[2]
    heads_dev = w_query.shape[1] // head_dim
    group_size = heads_dev // kv_dev
    page_len = prefix_cache.shape[1]
    rows_mdl = seq_len // lax.axis_size("mdl")
    group_idx = lax.axis_index("grp")
    tok_idx = lax.axis_index("tok")
    mdl_idx = lax.axis_index("mdl")
    tokens = hidden_in[0].astype(jnp.float32)
    squares = lax.psum(jnp.sum(tokens * tokens, -1), "mdl")
    normed = (tokens * lax.rsqrt(squares[:, None] / model_width + EPS) * attn_gain).astype(
        jnp.bfloat16
    )
    w_joined = jnp.concatenate([w_query, w_key, w_value], 1)
    partial_qkv = jnp.dot(
        lax.all_gather(normed, "tok", axis=0, tiled=True),
        w_joined,
        preferred_element_type=jnp.float32,
    )
    pages = lax.all_gather(
        prefix_cache.reshape(-1, kv_dev * 2 * head_dim), ("grp", "mdl"), axis=0, tiled=True
    )
    partial_qkv, pages = lax.optimization_barrier((partial_qkv, pages))
    qkv_rows = lax.psum_scatter(partial_qkv, "mdl", scatter_dimension=0, tiled=True)
    seg_row = lax.dynamic_index_in_dim(seg_ids, group_idx, 0, keepdims=False)
    prefix_row = lax.dynamic_index_in_dim(request_prefix, group_idx, 0, keepdims=False)
    requests = jnp.arange(req_count, dtype=jnp.int32)
    member = seg_row[:, None] == requests[None, :]
    counts = jnp.sum(member.astype(jnp.int32), 0)
    offsets = jnp.cumsum(counts) - counts
    row_start = mdl_idx * rows_mdl
    my_rows = row_start + jnp.arange(rows_mdl, dtype=jnp.int32)
    my_seg = lax.dynamic_slice_in_dim(seg_row, row_start, rows_mdl)
    my_member = my_seg[:, None] == requests[None, :]
    positions = PREFIX + my_rows - jnp.sum(jnp.where(my_member, offsets[None, :], 0), 1)
    my_prefix = jnp.sum(jnp.where(my_member, prefix_row[None, :], 0), 1)
    frequency = THETA ** (
        -(jnp.arange(head_dim // 2, dtype=jnp.float32) * 2.0 / head_dim)
    )
    angles = positions.astype(jnp.float32)[:, None] * frequency[None, :]
    cosine = jnp.cos(angles)
    sine = jnp.sin(angles)
    cosine = jnp.concatenate([cosine, cosine], 1)
    sine = jnp.concatenate([-sine, sine], 1)
    appended = rope_kv(qkv_rows, cosine, sine, heads_dev, kv_dev, head_dim)
    suffix = lax.all_gather(appended, "mdl", axis=0, tiled=True)
    attended = attend(
        qkv_rows, cosine, sine, my_seg, my_rows, my_prefix, seg_row, suffix, pages, page_table,
        kv_dev, group_size, head_dim, page_len,
    )
    partial_out = jnp.dot(
        lax.all_gather(attended, "mdl", axis=0, tiled=True),
        w_out,
        preferred_element_type=jnp.float32,
    )
    residual = tokens + lax.psum_scatter(
        partial_out.astype(jnp.bfloat16), "tok", scatter_dimension=0, tiled=True
    ).astype(jnp.float32)
    squares_ffn = lax.psum(jnp.sum(residual * residual, -1), "mdl")
    ffn_input = (residual * lax.rsqrt(squares_ffn[:, None] / model_width + EPS) * ffn_gain).astype(
        jnp.bfloat16
    )
    w_pair = jnp.concatenate([w_gate, w_up], 1)
    ff_dev = w_gate.shape[1]
    partial_ffn = jnp.dot(
        lax.all_gather(ffn_input, "tok", axis=0, tiled=True),
        w_pair,
        preferred_element_type=jnp.float32,
    )
    summed = lax.psum_scatter(
        partial_ffn.astype(jnp.bfloat16), "mdl", scatter_dimension=0, tiled=True
    ).astype(jnp.float32)
    activated = (jax.nn.silu(summed[:, :ff_dev]) * summed[:, ff_dev:]).astype(jnp.bfloat16)
    partial_down = jnp.dot(
        lax.all_gather(activated, "mdl", axis=0, tiled=True),
        w_down,
        preferred_element_type=jnp.float32,
    )
    final_rows = residual + lax.psum_scatter(
        partial_down.astype(jnp.bfloat16), "tok", scatter_dimension=0, tiled=True
    ).astype(jnp.float32)
    tok_start = tok_idx * tok_rows
    my_tok_rows = tok_start + jnp.arange(tok_rows, dtype=jnp.int32)
    tok_seg = lax.dynamic_slice_in_dim(seg_row, tok_start, tok_rows)
    row_squares = jnp.sum(final_rows * final_rows, -1)
    req_squares = jnp.sum(
        jnp.where(tok_seg[:, None] == requests[None, :], row_squares[:, None], 0.0), 0
    )
    ends = offsets + counts - 1
    picked = ends[:, None] == my_tok_rows[None, :]
    last_part = jnp.sum(jnp.where(picked[:, :, None], final_rows[None, :, :], 0.0), 1)
    half = req_count * feat_dev // 8
    width = -(-half // 128) * 128
    bundle = jnp.concatenate(
        [
            jnp.pad(last_part.reshape(8, half), ((0, 0), (0, width - half))),
            jnp.pad(req_squares[:, None], ((0, 8 - req_count), (0, 127))),
        ],
        1,
    )
    everyone = exchange(bundle, True)
    mdl_total = lax.axis_size("mdl")
    last_all = (
        everyone[:, :, :half]
        .reshape(groups_total, mdl_total, req_count, feat_dev)
        .transpose(0, 2, 1, 3)
        .reshape(groups_total * req_count, model_width)
    )
    squares_all = everyone[:, :req_count, width].reshape(groups_total, mdl_total, req_count)
    req_total = lax.dynamic_index_in_dim(jnp.sum(squares_all, 1), group_idx, 0, keepdims=False)
    req_norm = jnp.sqrt(req_total / (counts.astype(jnp.float32) * model_width) + EPS)
    last_normed = (
        last_all * lax.rsqrt(jnp.mean(last_all * last_all, -1, keepdims=True) + EPS) * final_gain
    ).astype(jnp.bfloat16)
    logits = lax.dot_general(
        last_normed, lm_head, (((1,), (1,)), ((), ())), preferred_element_type=jnp.float32
    )
    rows_all = groups_total * req_count
    best = jnp.broadcast_to(jnp.max(logits, -1)[:, None], (rows_all, 128))
    max_logit = exchange(best, False)[:, 0].reshape(groups_total, req_count)
    return (
        final_rows.astype(jnp.bfloat16)[None],
        appended.reshape(1, rows_mdl, kv_dev, 2 * head_dim),
        req_norm[None],
        max_logit,
        logits,
    )


def solution(mesh):
    return jax.shard_map(
        on_device,
        mesh=mesh,
        in_specs=(
            P("grp", "tok", "mdl"),
            P(),
            P(),
            P(),
            P(("grp", "mdl"), None, "tok", None),
            P("mdl"),
            P("mdl", "tok"),
            P("mdl", "tok"),
            P("mdl", "tok"),
            P("tok", "mdl"),
            P("mdl"),
            P("mdl", "tok"),
            P("mdl", "tok"),
            P("tok", "mdl"),
            P(),
            P(("grp", "tok", "mdl"), None),
        ),
        out_specs=(
            P("grp", "tok", "mdl"),
            P("grp", "mdl", "tok", None),
            P("grp", None),
            P(),
            P(None, ("grp", "tok", "mdl")),
        ),
        check_vma=False,
    )
```

```python
import functools

import jax
import jax.numpy as jnp
from jax import lax
from jax.experimental import pallas as pl
from jax.experimental.pallas import tpu as pltpu
from jax.sharding import PartitionSpec as P

PREFIX = 4096
PAGE = 256


EPS = 1e-06
THETA = 1000000.0
NEG = -1e30


MESH = pl.DeviceIdType.MESH
LOG2E = 1.4426950408889634


def turn(block, cosine, signed_sine):
    return block * cosine + pltpu.roll(block, block.shape[1] // 2, 1) * signed_sine


def rope_kv_body(k_ref, v_ref, cos_ref, sin_ref, out_ref):
    width = k_ref.shape[1]
    out_ref[:, :width] = turn(k_ref[...], cos_ref[...], sin_ref[...]).astype(jnp.bfloat16)
    out_ref[:, width:] = v_ref[...].astype(jnp.bfloat16)


def rope_kv(qkv_rows, cosine, sine, heads, kv_dev, head_dim):
    rows = qkv_rows.shape[0]
    return pl.pallas_call(
        rope_kv_body,
        grid=(kv_dev,),
        in_specs=[
            pl.BlockSpec((rows, head_dim), lambda c: (0, heads + c)),
            pl.BlockSpec((rows, head_dim), lambda c: (0, heads + kv_dev + c)),
            pl.BlockSpec((rows, head_dim), lambda c: (0, 0)),
            pl.BlockSpec((rows, head_dim), lambda c: (0, 0)),
        ],
        out_specs=pl.BlockSpec((rows, 2 * head_dim), lambda c: (0, c)),
        out_shape=jax.ShapeDtypeStruct((rows, kv_dev * 2 * head_dim), jnp.bfloat16),
    )(qkv_rows, qkv_rows, cosine, sine)


def attend_body(
    prefixes, pages_each, page_len, group_size, head_dim, together,
    table_ref, need_ref,
    q_ref, cos_ref, sin_ref, seg_ref, row_ref, prefix_ref, key_seg_ref, suffix_ref, pages_ref,
    out_ref,
):
    block = pl.program_id(1)
    toks = q_ref.shape[0]
    scale = head_dim ** (-0.5) * LOG2E
    contract = (((1,), (1,)), ((), ()))
    q = jnp.concatenate(
        [
            turn(q_ref[:, h * head_dim : (h + 1) * head_dim], cos_ref[...], sin_ref[...])
            for h in range(group_size)
        ],
        0,
    ).astype(jnp.bfloat16)
    stack = lambda column: jnp.concatenate([column] * group_size, 0)
    seg = stack(seg_ref[...])
    row = stack(row_ref[...])
    prefix = stack(prefix_ref[...])

    def fold(parts, op):
        width = head_dim
        pieces = [p[:, j : j + width] for p in parts for j in range(0, p.shape[1], width)]
        return functools.reduce(op, pieces)

    keys = suffix_ref[:, :head_dim]
    scores = lax.dot_general(q, keys, contract, preferred_element_type=jnp.float32) * scale
    index = lax.broadcasted_iota(jnp.int32, scores.shape, 1)
    scores = jnp.where((key_seg_ref[...] == seg) & (index <= row), scores, NEG)
    top = jnp.max(fold([scores], jnp.maximum), 1, keepdims=True)
    weights = jnp.exp2(scores - top)
    total = fold([weights], jnp.add)
    mixed = jnp.dot(
        weights.astype(jnp.bfloat16), suffix_ref[:, head_dim:], preferred_element_type=jnp.float32
    )
    for p in range(prefixes):
        seen = prefix == p

        def step(i, carry):
            top, total, mixed = carry
            starts = [
                pl.multiple_of(
                    table_ref[p * pages_each + i * together + u] * page_len, page_len
                )
                for u in range(together)
            ]
            scores = [
                lax.dot_general(
                    q,
                    pages_ref[pl.ds(start, page_len), :head_dim],
                    contract,
                    preferred_element_type=jnp.float32,
                )
                for start in starts
            ]
            best = jnp.max(fold(scores, jnp.maximum), 1, keepdims=True) * scale
            new_top = jnp.where(seen, jnp.maximum(top, best), top)
            shift = jnp.where(seen, new_top, -NEG)
            factor = jnp.exp2(top - new_top)
            weights = [jnp.exp2(s * scale - shift) for s in scores]
            total = total * factor + fold(weights, jnp.add)
            mixed = mixed * factor
            for start, w in zip(starts, weights):
                mixed = mixed + jnp.dot(
                    w.astype(jnp.bfloat16),
                    pages_ref[pl.ds(start, page_len), head_dim:],
                    preferred_element_type=jnp.float32,
                )
            return new_top, total, mixed

        trips = need_ref[block * prefixes + p] * (pages_each // together)
        top, total, mixed = lax.fori_loop(0, trips, step, (top, total, mixed))
    result = (mixed / jnp.sum(total, 1, keepdims=True)).astype(jnp.bfloat16)
    for h in range(group_size):
        out_ref[:, h * head_dim : (h + 1) * head_dim] = result[h * toks : (h + 1) * toks]


def attend(
    qkv_rows, cosine, sine, my_seg, my_rows, my_prefix, seg_row, suffix, pages, page_table,
    kv_dev, group_size, head_dim, page_len,
):
    rows = qkv_rows.shape[0]
    toks = 64
    blocks = rows // toks
    pages_each = PREFIX // PAGE
    prefixes = page_table.shape[0] // pages_each
    need = jnp.max(
        (my_prefix.reshape(blocks, toks)[:, None, :] == jnp.arange(prefixes)[None, :, None]).astype(
            jnp.int32
        ),
        -1,
    ).reshape(-1)
    seq_len = suffix.shape[0]
    q_width = group_size * head_dim
    by_row = lambda c, b, *_: (b, 0)
    by_kv = lambda c, b, *_: (0, c)
    by_both = lambda c, b, *_: (b, c)
    body = functools.partial(
        attend_body, prefixes, pages_each, page_len, group_size, head_dim, 4
    )
    elements = rows * kv_dev * group_size * (PREFIX + seq_len)
    return pl.pallas_call(
        body,
        grid_spec=pltpu.PrefetchScalarGridSpec(
            num_scalar_prefetch=2,
            grid=(kv_dev, blocks),
            in_specs=[
                pl.BlockSpec((toks, q_width), by_both),
                pl.BlockSpec((toks, head_dim), by_row),
                pl.BlockSpec((toks, head_dim), by_row),
                pl.BlockSpec((toks, 1), by_row),
                pl.BlockSpec((toks, 1), by_row),
                pl.BlockSpec((toks, 1), by_row),
                pl.BlockSpec((1, seq_len), lambda c, b, *_: (0, 0)),
                pl.BlockSpec((seq_len, 2 * head_dim), by_kv),
                pl.BlockSpec((pages.shape[0], 2 * head_dim), by_kv),
            ],
            out_specs=pl.BlockSpec((toks, q_width), by_both),
        ),
        out_shape=jax.ShapeDtypeStruct((rows, kv_dev * q_width), jnp.bfloat16),
        compiler_params=pltpu.CompilerParams(vmem_limit_bytes=48 * 1024 * 1024),
        cost_estimate=pl.CostEstimate(
            flops=4 * head_dim * elements, bytes_accessed=pages.size * 2, transcendentals=elements
        ),
    )(
        page_table, need, qkv_rows, cosine, sine, my_seg[:, None], my_rows[:, None],
        my_prefix[:, None], seg_row[None, :], suffix, pages,
    )


def exchange_body(
    sizes, summing,
    x_ref, out_ref, tok_slots, stage, all_slots, tok_send, tok_recv, all_send, all_recv,
):
    grp_n, tok_n, mdl_n = sizes
    g, t, m = (lax.axis_index(name) for name in ("grp", "tok", "mdl"))
    tok_peers = [
        (d, {"tok": lax.rem(t + d, tok_n)}) for d in range(1, tok_n)
    ]
    plane_peers = [
        (
            gd * mdl_n + md,
            {"grp": lax.rem(g + gd, grp_n), "mdl": lax.rem(m + md, mdl_n)},
        )
        for gd in range(grp_n)
        for md in range(mdl_n)
        if gd + md > 0
    ]
    barrier = pltpu.get_barrier_semaphore()
    for _, peer in tok_peers + plane_peers:
        pl.semaphore_signal(barrier, inc=1, device_id=peer, device_id_type=MESH)
    pl.semaphore_wait(barrier, len(tok_peers) + len(plane_peers))

    def spread(source, slots, mine, peers, send, recv):
        copies = [
            pltpu.make_async_remote_copy(
                src_ref=source,
                dst_ref=slots.at[mine],
                send_sem=send.at[d],
                recv_sem=recv.at[d],
                device_id=peer,
                device_id_type=MESH,
            )
            for d, peer in peers
        ]
        for copy in copies:
            copy.start()
        slots[mine] = source[...]
        for copy in copies:
            copy.wait()

    join = jnp.add if summing else jnp.maximum
    spread(x_ref, tok_slots, t, tok_peers, tok_send, tok_recv)
    stage[...] = functools.reduce(join, [tok_slots[k] for k in range(tok_n)])
    spread(stage, all_slots, g * mdl_n + m, plane_peers, all_send, all_recv)
    if summing:
        out_ref[...] = all_slots[...]
    else:
        out_ref[...] = functools.reduce(join, [all_slots[k] for k in range(grp_n * mdl_n)])


def exchange(values, summing):
    sizes = tuple(lax.axis_size(name) for name in ("grp", "tok", "mdl"))
    plane = sizes[0] * sizes[2]
    shape = values.shape
    return pl.pallas_call(
        functools.partial(exchange_body, sizes, summing),
        out_shape=jax.ShapeDtypeStruct((plane,) + shape if summing else shape, jnp.float32),
        in_specs=[pl.BlockSpec(memory_space=pltpu.VMEM)],
        out_specs=pl.BlockSpec(memory_space=pltpu.VMEM),
        scratch_shapes=[
            pltpu.VMEM((sizes[1],) + shape, jnp.float32),
            pltpu.VMEM(shape, jnp.float32),
            pltpu.VMEM((plane,) + shape, jnp.float32),
            pltpu.SemaphoreType.DMA((sizes[1],)),
            pltpu.SemaphoreType.DMA((sizes[1],)),
            pltpu.SemaphoreType.DMA((plane,)),
            pltpu.SemaphoreType.DMA((plane,)),
        ],
        compiler_params=pltpu.CompilerParams(
            collective_id=1 if summing else 2, has_side_effects=True
        ),
    )(values)


def gather_body(
    sizes, x_ref, pages_ref, x_out, pages_out,
    own_sem, tok_send, tok_recv, grp_send, grp_recv, mdl_send, mdl_recv,
):
    grp_n, tok_n, mdl_n = sizes
    g, t, m = (lax.axis_index(name) for name in ("grp", "tok", "mdl"))
    grp_peers = [{"grp": lax.rem(g + d, grp_n)} for d in range(1, grp_n)]
    tok_peers = [{"tok": lax.rem(t + d, tok_n)} for d in range(1, tok_n)]
    mdl_peers = [{"mdl": lax.rem(m + d, mdl_n)} for d in range(1, mdl_n)]
    barrier = pltpu.get_barrier_semaphore()
    for peer in grp_peers + tok_peers + mdl_peers:
        pl.semaphore_signal(barrier, inc=1, device_id=peer, device_id_type=MESH)
    pl.semaphore_wait(barrier, grp_n + tok_n + mdl_n - 3)

    def send(source, target, send_sem, recv_sem, peer):
        copy = pltpu.make_async_remote_copy(
            src_ref=source,
            dst_ref=target,
            send_sem=send_sem,
            recv_sem=recv_sem,
            device_id=peer,
            device_id_type=MESH,
        )
        copy.start()
        return copy

    from_grp = [
        send(pages_ref, pages_out.at[g, m], grp_send.at[d], grp_recv.at[d], peer)
        for d, peer in enumerate(grp_peers)
    ]
    from_tok = [
        send(x_ref, x_out.at[t], tok_send.at[d], tok_recv.at[d], peer)
        for d, peer in enumerate(tok_peers)
    ]
    from_mdl = [
        send(pages_ref, pages_out.at[g, m], mdl_send.at[0, d], mdl_recv.at[0, d], peer)
        for d, peer in enumerate(mdl_peers)
    ]
    own = [
        pltpu.make_async_copy(x_ref, x_out.at[t], own_sem.at[0]),
        pltpu.make_async_copy(pages_ref, pages_out.at[g, m], own_sem.at[1]),
    ]
    for copy in own:
        copy.start()
    for d, copy in enumerate(from_grp):
        copy.wait_recv()
        held = pages_out.at[lax.rem(g + grp_n - 1 - d, grp_n), m]
        for e, peer in enumerate(mdl_peers):
            from_mdl.append(send(held, held, mdl_send.at[d + 1, e], mdl_recv.at[d + 1, e], peer))
    for copy in own:
        copy.wait()
    for copy in from_grp:
        copy.wait_send()
    for copy in from_tok + from_mdl:
        copy.wait()


def gather_rows_and_pages(x, pages):
    sizes = tuple(lax.axis_size(name) for name in ("grp", "tok", "mdl"))
    grp_n, tok_n, mdl_n = sizes
    anywhere = pl.BlockSpec(memory_space=pl.ANY)
    dma = pltpu.SemaphoreType.DMA
    rows, all_pages = pl.pallas_call(
        functools.partial(gather_body, sizes),
        out_shape=(
            jax.ShapeDtypeStruct((tok_n,) + x.shape, x.dtype),
            jax.ShapeDtypeStruct((grp_n, mdl_n) + pages.shape, pages.dtype),
        ),
        in_specs=[anywhere, anywhere],
        out_specs=(anywhere, anywhere),
        scratch_shapes=[
            dma((2,)),
            dma((tok_n,)), dma((tok_n,)),
            dma((grp_n,)), dma((grp_n,)),
            dma((grp_n, mdl_n)), dma((grp_n, mdl_n)),
        ],
        compiler_params=pltpu.CompilerParams(collective_id=3, has_side_effects=True),
    )(x, pages)
    return rows.reshape(-1, x.shape[1]), all_pages.reshape(-1, pages.shape[1])


def swap_cores(x):
    return lax.ppermute(x, "mdl", [(0, 1), (1, 0)])


def gather_mdl(x):
    if lax.axis_size("mdl") != 2:
        return lax.all_gather(x, "mdl", axis=0, tiled=True)
    other = swap_cores(x)
    first = lax.axis_index("mdl") == 0
    return jnp.concatenate([jnp.where(first, x, other), jnp.where(first, other, x)], 0)


def scatter_mdl(x):
    if lax.axis_size("mdl") != 2:
        return lax.psum_scatter(x, "mdl", scatter_dimension=0, tiled=True).astype(jnp.float32)
    rows = x.shape[0] // 2
    m = lax.axis_index("mdl")
    theirs = swap_cores(lax.dynamic_slice_in_dim(x, (1 - m) * rows, rows))
    mine = lax.dynamic_slice_in_dim(x, m * rows, rows)
    return mine.astype(jnp.float32) + theirs.astype(jnp.float32)


def on_device(
    hidden_in,
    seg_ids,
    request_prefix,
    page_table,
    prefix_cache,
    attn_gain,
    w_query,
    w_key,
    w_value,
    w_out,
    ffn_gain,
    w_gate,
    w_up,
    w_down,
    final_gain,
    lm_head,
):
    groups_total = seg_ids.shape[0]
    seq_len = seg_ids.shape[1]
    req_count = request_prefix.shape[1]
    tok_rows = hidden_in.shape[1]
    feat_dev = hidden_in.shape[2]
    model_width = feat_dev * lax.axis_size("mdl")
    head_dim = prefix_cache.shape[3] // 2
    kv_dev = prefix_cache.shape[2]
    heads_dev = w_query.shape[1] // head_dim
    group_size = heads_dev // kv_dev
    page_len = prefix_cache.shape[1]
    rows_mdl = seq_len // lax.axis_size("mdl")
    group_idx = lax.axis_index("grp")
    tok_idx = lax.axis_index("tok")
    mdl_idx = lax.axis_index("mdl")
    tokens = hidden_in[0].astype(jnp.float32)
    squares = lax.psum(jnp.sum(tokens * tokens, -1), "mdl")
    normed = (tokens * lax.rsqrt(squares[:, None] / model_width + EPS) * attn_gain).astype(
        jnp.bfloat16
    )
    w_joined = jnp.concatenate([w_query, w_key, w_value], 1)
    all_normed, pages = gather_rows_and_pages(
        normed, prefix_cache.reshape(-1, kv_dev * 2 * head_dim)
    )
    partial_qkv = jnp.dot(
        all_normed,
        w_joined,
        preferred_element_type=jnp.float32,
    )
    qkv_rows = scatter_mdl(partial_qkv)
    seg_row = lax.dynamic_index_in_dim(seg_ids, group_idx, 0, keepdims=False)
    prefix_row = lax.dynamic_index_in_dim(request_prefix, group_idx, 0, keepdims=False)
    requests = jnp.arange(req_count, dtype=jnp.int32)
    member = seg_row[:, None] == requests[None, :]
    counts = jnp.sum(member.astype(jnp.int32), 0)
    offsets = jnp.cumsum(counts) - counts
    row_start = mdl_idx * rows_mdl
    my_rows = row_start + jnp.arange(rows_mdl, dtype=jnp.int32)
    my_seg = lax.dynamic_slice_in_dim(seg_row, row_start, rows_mdl)
    my_member = my_seg[:, None] == requests[None, :]
    positions = PREFIX + my_rows - jnp.sum(jnp.where(my_member, offsets[None, :], 0), 1)
    my_prefix = jnp.sum(jnp.where(my_member, prefix_row[None, :], 0), 1)
    frequency = THETA ** (
        -(jnp.arange(head_dim // 2, dtype=jnp.float32) * 2.0 / head_dim)
    )
    angles = positions.astype(jnp.float32)[:, None] * frequency[None, :]
    cosine = jnp.cos(angles)
    sine = jnp.sin(angles)
    cosine = jnp.concatenate([cosine, cosine], 1)
    sine = jnp.concatenate([-sine, sine], 1)
    appended = rope_kv(qkv_rows, cosine, sine, heads_dev, kv_dev, head_dim)
    suffix = lax.all_gather(appended, "mdl", axis=0, tiled=True)
    attended = attend(
        qkv_rows, cosine, sine, my_seg, my_rows, my_prefix, seg_row, suffix, pages, page_table,
        kv_dev, group_size, head_dim, page_len,
    )
    partial_out = jnp.dot(
        gather_mdl(attended),
        w_out,
        preferred_element_type=jnp.float32,
    )
    residual = tokens + lax.psum_scatter(
        partial_out.astype(jnp.bfloat16), "tok", scatter_dimension=0, tiled=True
    ).astype(jnp.float32)
    squares_ffn = lax.psum(jnp.sum(residual * residual, -1), "mdl")
    ffn_input = (residual * lax.rsqrt(squares_ffn[:, None] / model_width + EPS) * ffn_gain).astype(
        jnp.bfloat16
    )
    w_pair = jnp.concatenate([w_gate, w_up], 1)
    ff_dev = w_gate.shape[1]
    partial_ffn = jnp.dot(
        lax.all_gather(ffn_input, "tok", axis=0, tiled=True),
        w_pair,
        preferred_element_type=jnp.float32,
    )
    summed = scatter_mdl(partial_ffn.astype(jnp.bfloat16))
    activated = (jax.nn.silu(summed[:, :ff_dev]) * summed[:, ff_dev:]).astype(jnp.bfloat16)
    partial_down = jnp.dot(
        gather_mdl(activated),
        w_down,
        preferred_element_type=jnp.float32,
    )
    final_rows = residual + lax.psum_scatter(
        partial_down.astype(jnp.bfloat16), "tok", scatter_dimension=0, tiled=True
    ).astype(jnp.float32)
    tok_start = tok_idx * tok_rows
    my_tok_rows = tok_start + jnp.arange(tok_rows, dtype=jnp.int32)
    tok_seg = lax.dynamic_slice_in_dim(seg_row, tok_start, tok_rows)
    row_squares = jnp.sum(final_rows * final_rows, -1)
    req_squares = jnp.sum(
        jnp.where(tok_seg[:, None] == requests[None, :], row_squares[:, None], 0.0), 0
    )
    ends = offsets + counts - 1
    picked = ends[:, None] == my_tok_rows[None, :]
    last_part = jnp.sum(jnp.where(picked[:, :, None], final_rows[None, :, :], 0.0), 1)
    half = req_count * feat_dev // 8
    width = -(-half // 128) * 128
    bundle = jnp.concatenate(
        [
            jnp.pad(last_part.reshape(8, half), ((0, 0), (0, width - half))),
            jnp.pad(req_squares[:, None], ((0, 8 - req_count), (0, 127))),
        ],
        1,
    )
    everyone = exchange(bundle, True)
    mdl_total = lax.axis_size("mdl")
    last_all = (
        everyone[:, :, :half]
        .reshape(groups_total, mdl_total, req_count, feat_dev)
        .transpose(0, 2, 1, 3)
        .reshape(groups_total * req_count, model_width)
    )
    squares_all = everyone[:, :req_count, width].reshape(groups_total, mdl_total, req_count)
    req_total = lax.dynamic_index_in_dim(jnp.sum(squares_all, 1), group_idx, 0, keepdims=False)
    req_norm = jnp.sqrt(req_total / (counts.astype(jnp.float32) * model_width) + EPS)
    last_normed = (
        last_all * lax.rsqrt(jnp.mean(last_all * last_all, -1, keepdims=True) + EPS) * final_gain
    ).astype(jnp.bfloat16)
    logits = lax.dot_general(
        last_normed, lm_head, (((1,), (1,)), ((), ())), preferred_element_type=jnp.float32
    )
    rows_all = groups_total * req_count
    best = jnp.broadcast_to(jnp.max(logits, -1)[:, None], (rows_all, 128))
    max_logit = exchange(best, False)[:, 0].reshape(groups_total, req_count)
    return (
        final_rows.astype(jnp.bfloat16)[None],
        appended.reshape(1, rows_mdl, kv_dev, 2 * head_dim),
        req_norm[None],
        max_logit,
        logits,
    )


def solution(mesh):
    return jax.shard_map(
        on_device,
        mesh=mesh,
        in_specs=(
            P("grp", "tok", "mdl"),
            P(),
            P(),
            P(),
            P(("grp", "mdl"), None, "tok", None),
            P("mdl"),
            P("mdl", "tok"),
            P("mdl", "tok"),
            P("mdl", "tok"),
            P("tok", "mdl"),
            P("mdl"),
            P("mdl", "tok"),
            P("mdl", "tok"),
            P("tok", "mdl"),
            P(),
            P(("grp", "tok", "mdl"), None),
        ),
        out_specs=(
            P("grp", "tok", "mdl"),
            P("grp", "mdl", "tok", None),
            P("grp", None),
            P(),
            P(None, ("grp", "tok", "mdl")),
        ),
        check_vma=False,
    )
```
